32 devices in a mesh: seq: 4 (over y, x), dp: 8 (over z, core).
Axes of the slice: x: 2, y: 2, z: 4, core: 2. Of those that a mesh axis runs over, the one named last changes fastest.
Arguments:
- video_qkv: bfloat16 [8, 512, 3, 2048], P('dp', 'seq'), may hold values from -6 to 6
- video_cotangent: bfloat16 [8, 512, 2048], P('dp', 'seq'), may hold values from -192 to 192
- prompt_states: bfloat16 [8, 128, 4096], P('dp', None, 'seq'), may hold values from -6 to 6
- text_weight: bfloat16 [4096, 6144], P('seq', 'dp'), may hold values from -0.09375 to 0.09375
- text_cotangent: bfloat16 [8, 128, 2048], P('dp', None, 'seq'), may hold values from -192 to 192
- gain_query: float32 [16, 128], P('seq'), may hold values from 0.25 to 1.75
- gain_key: float32 [16, 128], P('seq'), may hold values from 0.25 to 1.75
- prompt_lengths: int32 [8], P('dp'), may hold values from 16 to 128
- prompt_source: int32 [8], replicated, may hold values from 0 to 7, each once
Outputs:
- grad_video_qkv: bfloat16 [8, 512, 3, 2048], P('dp', 'seq')
- grad_text_qkv: bfloat16 [8, 128, 6144], P('dp', None, 'seq')
The draws below stay inside these ranges and needn't reach their ends.
Inputs may be any that keep to these rules, and one draw needn't show every extreme that they name: prompt_source is a permutation: every row of prompt_states is the prompt of exactly one clip. Clip c's valid prompt rows are its first prompt_lengths[c] rows.
All inputs are finite; a program needn't handle non-finite values.
Results may differ from the reference program's by a relative error of at most 0.0091.
Values may be sent and summed in bfloat16 or wider, within the bound.
A program may use at most 64 MiB of HBM per device.

```python
import math
import jax
import jax.numpy as jnp
from jax import lax

HEADS = 16
HD = 128
T5W = 4096
PROMPT = 128
TOKENS = 512
CLIPS = 8
QKV = 6144


def plant(result, own_key, smallest, top_value):
    longest = result.shape.index(max(result.shape))
    spots = []
    for shift in (0, 1):
        where = [jax.random.randint(jax.random.fold_in(own_key, axis), (), 0, length) for axis, length in enumerate(result.shape)]
        where[longest] = (where[longest] + shift) % result.shape[longest]
        spots.append(tuple(where))
    return result.at[spots[0]].set(smallest).at[spots[1]].set(top_value)


def level_of(rng, dims, cuts, least, high):
    def one(position, parts):
        heights = jax.random.uniform(jax.random.fold_in(jax.random.fold_in(rng, 6), position), (parts,), jnp.float32, least / len(cuts), high / len(cuts))
        return jnp.repeat(jnp.exp(heights), dims[position] // parts).reshape((-1,) + (1,) * (len(dims) - position - 1))

    factor_of = one(*cuts[0])
    for cut in cuts[1:]:
        factor_of = factor_of * one(*cut)
    return factor_of


def scatter_about(rng, shape, spread, bound, split=(), held_as=jnp.bfloat16):
    level = level_of(rng, shape, split, -0.22, 0.18) if split else 1.0
    array = jax.random.normal(rng, shape, jnp.float32) * spread * level
    return jnp.minimum(jnp.maximum(array, -bound), bound).astype(held_as)


def setup_inputs(seed: int = 0) -> dict:
    keys = jax.random.split(jax.random.key(seed), 10)
    return {
        "video_qkv": scatter_about(keys[0], (CLIPS, TOKENS, 3, HEADS * HD), 1.0, 6.0, ((0, 8), (1, 4))),
        "video_cotangent": scatter_about(keys[1], (CLIPS, TOKENS, HEADS * HD), 32, 192.0, ((0, 8), (1, 4))),
        "prompt_states": scatter_about(keys[2], (CLIPS, PROMPT, T5W), 1.0, 6.0, ((0, 8), (2, 4))),
        "text_weight": scatter_about(keys[3], (T5W, QKV), T5W ** -0.5, 0.09375, ((0, 4), (1, 8))),
        "text_cotangent": scatter_about(keys[4], (CLIPS, PROMPT, HEADS * HD), 32, 192.0, ((0, 8), (2, 4))),
        "gain_query": jnp.clip(1.0 + 0.15 * jax.random.normal(keys[5], (HEADS, HD), jnp.float32), 0.25, 1.75),
        "gain_key": jnp.clip(1.0 + 0.15 * jax.random.normal(keys[6], (HEADS, HD), jnp.float32), 0.25, 1.75),
        "prompt_lengths": plant(jax.random.randint(keys[7], (CLIPS,), max(1, PROMPT // 8), PROMPT + 1), jax.random.fold_in(keys[7], 1), max(1, PROMPT // 8), PROMPT).astype(jnp.int32),
        "prompt_source": jax.random.permutation(keys[8], CLIPS).astype(jnp.int32),
    }


EPS = 1e-06

def rms_scale(values, gain):
    return values * lax.rsqrt(lax.optimization_barrier(jnp.mean(values * values, axis=-1, keepdims=True)) + EPS) * gain

def block_grads(query_normed, key_normed, values, upstream, key_valid):
    scale = 1.0 / math.sqrt(query_normed.shape[-1])
    scores = jnp.dot(query_normed, key_normed.T, preferred_element_type=jnp.float32) * scale
    weights = jnp.exp(scores) * key_valid
    probs = weights / lax.optimization_barrier(jnp.sum(weights, axis=-1, keepdims=True))
    probs_low = probs.astype(jnp.bfloat16)
    grad_probs = jnp.dot(upstream, values.T, preferred_element_type=jnp.float32)
    delta = lax.optimization_barrier(jnp.sum(probs * grad_probs, axis=-1, keepdims=True))
    grad_scores = (probs * (grad_probs - delta) * scale).astype(jnp.bfloat16)
    grad_query = jnp.dot(grad_scores, key_normed, preferred_element_type=jnp.float32)
    grad_key = jnp.dot(grad_scores.T, query_normed, preferred_element_type=jnp.float32)
    grad_value = jnp.dot(probs_low.T, upstream, preferred_element_type=jnp.float32)
    return (grad_query, grad_key, grad_value)

def norm_grad(raw, gain, cotangent):
    unused, pull = jax.vjp(lambda inner: rms_scale(inner, gain), raw)
    return pull(cotangent)[0]

def reference(video_qkv, video_cotangent, prompt_states, text_weight, text_cotangent, gain_query, gain_key, prompt_lengths, prompt_source):

    def one_clip(clip):
        source = lax.dynamic_index_in_dim(prompt_source, clip, 0, keepdims=False).astype(jnp.int32)
        prompt = lax.dynamic_index_in_dim(prompt_states, source, 0, keepdims=False)
        text_qkv = jnp.dot(prompt, text_weight, preferred_element_type=jnp.float32).astype(jnp.bfloat16)
        text_heads = jnp.transpose(text_qkv.reshape(PROMPT, HEADS, 3, HD), (1, 2, 0, 3))
        video = lax.dynamic_index_in_dim(video_qkv, clip, 0, keepdims=False)
        video_heads = jnp.transpose(video.reshape(TOKENS, 3, HEADS, HD), (2, 1, 0, 3))
        upstream_video = jnp.transpose(lax.dynamic_index_in_dim(video_cotangent, clip, 0, keepdims=False).reshape(TOKENS, HEADS, HD), (1, 0, 2))
        upstream_text = jnp.transpose(lax.dynamic_index_in_dim(text_cotangent, clip, 0, keepdims=False).reshape(PROMPT, HEADS, HD), (1, 0, 2))
        length = lax.dynamic_index_in_dim(prompt_lengths, clip, 0, keepdims=False)
        key_valid = jnp.concatenate([jnp.ones((TOKENS,), jnp.float32), (jnp.arange(PROMPT, dtype=jnp.int32) < length).astype(jnp.float32)])

        def one_head(inputs):
            video_part, text_part, up_video, up_text, gain_q, gain_k = inputs
            query_raw = jnp.concatenate([video_part[0], text_part[0]], 0).astype(jnp.float32)
            key_raw = jnp.concatenate([video_part[1], text_part[1]], 0).astype(jnp.float32)
            values = jnp.concatenate([video_part[2], text_part[2]], 0)
            upstream = jnp.concatenate([up_video, up_text], 0)
            query_normed = rms_scale(query_raw, gain_q).astype(jnp.bfloat16)
            key_normed = rms_scale(key_raw, gain_k).astype(jnp.bfloat16)
            grad_qn, grad_kn, grad_value = block_grads(query_normed, key_normed, values, upstream, key_valid)
            grad_query = norm_grad(query_raw, gain_q, grad_qn)
            grad_key = norm_grad(key_raw, gain_k, grad_kn)
            return jnp.stack([grad_query, grad_key, grad_value], 0).astype(jnp.bfloat16)
        grads = lax.map(one_head, (video_heads, text_heads, upstream_video, upstream_text, gain_query, gain_key))
        video_grad = jnp.transpose(grads[:, :, :TOKENS], (2, 1, 0, 3)).reshape(TOKENS, 3, HEADS * HD)
        text_grad = jnp.transpose(grads[:, :, TOKENS:], (2, 0, 1, 3)).reshape(PROMPT, QKV)
        return (video_grad, text_grad)
    grad_video_qkv, grad_text_qkv = lax.map(one_clip, jnp.arange(CLIPS, dtype=jnp.int32))
    return (grad_video_qkv, grad_text_qkv)
```

```python
import functools
import math

import jax
import jax.numpy as jnp
from jax import lax
from jax.experimental import pallas as pl
from jax.experimental.pallas import tpu as pltpu
from jax.sharding import PartitionSpec as P

EPS = 1e-06
BF = jnp.bfloat16
F32 = jnp.float32


def dot_nt(a, b):
    return lax.dot_general(a, b, (((1,), (1,)), ((), ())), preferred_element_type=F32)


def dot_nn(a, b):
    return jnp.dot(a, b, preferred_element_type=F32)


def kernel(
    seq,
    dp,
    blk,
    qkv,
    cot,
    states,
    weight,
    up_text,
    gain_q,
    gain_k,
    length,
    source,
    out,
    out_text,
    xall,
    wbuf,
    vbuf,
    pbuf,
    rbuf,
    sums,
    zbuf,
    tbuf,
    tfull,
    qn_s,
    u_s,
    dq_s,
    dk_s,
    dv_s,
    gbuf,
    x_send,
    f_send,
    x_recv,
    v_send,
    v_recv,
    r_send,
    r_recv,
    z_send,
    z_recv,
    t_send,
    t_recv,
    o_send,
    o_recv,
    l_sem,
):
    ms = lax.axis_index("seq")
    md = lax.axis_index("dp")
    heads = gain_q.shape[0]
    hd = gain_q.shape[1]
    tok = qkv.shape[1]
    tokens = seq * tok
    prompt = states.shape[0]
    part = prompt // seq
    cols = weight.shape[1]
    per = dp // seq
    width = heads * hd
    half = dp // 2
    partner = md + 1 - 2 * lax.rem(md, 2)

    def seq_peer(i):
        return lax.rem(ms + i, seq)

    def dp_peer(i):
        return lax.rem(md + i, dp)

    def remote(src, dst, send, recv, where):
        return pltpu.make_async_remote_copy(
            src_ref=src,
            dst_ref=dst,
            send_sem=send,
            recv_sem=recv,
            device_id=where,
            device_id_type=pl.DeviceIdType.MESH,
        )

    barrier = pltpu.get_barrier_semaphore()
    for i in range(1, seq):
        pl.semaphore_signal(
            barrier, inc=1, device_id={"seq": seq_peer(i)}, device_id_type=pl.DeviceIdType.MESH
        )
    for i in range(1, dp):
        pl.semaphore_signal(
            barrier, inc=1, device_id={"dp": dp_peer(i)}, device_id_type=pl.DeviceIdType.MESH
        )

    def rows_of(s):
        return pl.ds(pl.multiple_of(s * tok, tok), tok)

    def width_of(s):
        return pl.ds(pl.multiple_of(s * width, width), width)

    local_x = pltpu.make_async_copy(states, xall.at[md], l_sem.at[0])
    local_w = pltpu.make_async_copy(weight, wbuf, l_sem.at[1])
    local_v = pltpu.make_async_copy(
        qkv.at[:, :, width_of(ms)], vbuf.at[pl.ds(0, 3), rows_of(ms), :], l_sem.at[2]
    )
    local_u = pltpu.make_async_copy(
        cot.at[:, width_of(ms)], vbuf.at[3, rows_of(ms), :], l_sem.at[3]
    )
    local_x.start()
    local_w.start()
    local_v.start()
    local_u.start()
    pl.semaphore_wait(barrier, seq - 1 + dp - 1)

    def x_copy(i):
        return remote(
            states, xall.at[md], x_send.at[i], x_recv.at[md], {"dp": dp_peer(2 * i)}
        )

    def forward(g, src):
        return remote(src, xall.at[g], f_send.at[g], x_recv.at[g], {"dp": partner})

    def x_arrived(g):
        remote(states, xall.at[g], x_send.at[0], x_recv.at[g], {"dp": partner}).wait_recv()

    for i in range(1, half):
        x_copy(i).start()
    forward(md, states).start()

    def v_copy(i):
        to = seq_peer(i)
        return remote(
            qkv.at[:, :, width_of(to)],
            vbuf.at[pl.ds(0, 3), rows_of(ms), :],
            v_send.at[i, 0],
            v_recv.at[ms, 0],
            {"seq": to},
        )

    def u_copy(i):
        to = seq_peer(i)
        return remote(
            cot.at[:, width_of(to)],
            vbuf.at[3, rows_of(ms), :],
            v_send.at[i, 1],
            v_recv.at[ms, 1],
            {"seq": to},
        )

    for i in range(1, seq):
        v_copy(i).start()
        u_copy(i).start()

    for i in range(1, half):
        g = lax.rem(md + dp - 2 * i, dp)
        x_arrived(g)
        forward(g, xall.at[g]).start()
    for i in range(half):
        x_arrived(lax.rem(partner + dp - 2 * i, dp))
    local_x.wait()
    local_w.wait()

    def r_copy(c, i):
        to = seq_peer(i)
        return remote(
            pbuf.at[to, c], rbuf.at[ms, c], r_send.at[i, c], r_recv.at[ms, c], {"seq": to}
        )

    def project(n, carry):
        c = dp_peer(n)
        value = dot_nn(xall[source[c]], wbuf[...])
        for q in range(seq):
            pbuf[q, c] = value[q * part : (q + 1) * part].astype(BF)
        for i in range(1, seq):
            r_copy(c, i).start()
        return carry

    lax.fori_loop(0, dp, project, 0)

    def z_copy(c):
        return remote(sums.at[c], zbuf.at[md], z_send.at[c], z_recv.at[md], {"dp": c})

    def reduced(c):
        total = pbuf[ms, c].astype(F32)
        for i in range(1, seq):
            s = seq_peer(i)
            remote(
                pbuf.at[s, c], rbuf.at[s, c], r_send.at[i, c], r_recv.at[s, c], {"seq": s}
            ).wait_recv()
            total = total + rbuf[s, c].astype(F32)
        return total.astype(BF)

    zbuf[md] = reduced(md)

    def reduce_step(n, carry):
        c = dp_peer(n)
        sums[c] = reduced(c)
        z_copy(c).start()
        return carry

    lax.fori_loop(1, dp, reduce_step, 0)

    def z_arrived(n):
        g = dp_peer(n)
        remote(sums.at[g], zbuf.at[g], z_send.at[g], z_recv.at[g], {"dp": g}).wait_recv()

    for n in range(1, dp):
        z_arrived(dp - n)

    def t_copy(i):
        to = seq_peer(i)
        return remote(
            zbuf.at[pl.ds(to * per, per)], tbuf.at[ms], t_send.at[i], t_recv.at[ms], {"seq": to}
        )

    for i in range(1, seq):
        t_copy(i).start()
    tbuf[ms] = zbuf[pl.ds(ms * per, per)]
    for i in range(1, seq):
        s = seq_peer(i)
        remote(
            zbuf.at[pl.ds(0, per)], tbuf.at[s], t_send.at[i], t_recv.at[s], {"seq": s}
        ).wait_recv()
        remote(
            qkv.at[:, :, width_of(s)],
            vbuf.at[pl.ds(0, 3), rows_of(s), :],
            v_send.at[i, 0],
            v_recv.at[s, 0],
            {"seq": s},
        ).wait_recv()
        remote(
            cot.at[:, width_of(s)],
            vbuf.at[3, rows_of(s), :],
            v_send.at[i, 1],
            v_recv.at[s, 1],
            {"seq": s},
        ).wait_recv()
    local_v.wait()
    local_u.wait()
    for s in range(seq):
        for k in range(per):
            tfull[s * part : (s + 1) * part, k * cols : (k + 1) * cols] = tbuf[s, k].astype(F32)

    rows = tokens + prompt
    scale = 1.0 / math.sqrt(hd)
    valid = lax.broadcasted_iota(jnp.int32, (prompt, blk), 0) < length[0]

    def inverse(x):
        return lax.rsqrt(jnp.mean(x * x, axis=-1, keepdims=True) + EPS)

    def norm_back(x, r, gain, grad):
        scaled = grad * gain
        inner = jnp.mean(scaled * x, axis=-1, keepdims=True)
        return r * scaled - x * (r * r * r * inner)

    def o_copy(h, i):
        to = seq_peer(i)
        return remote(
            gbuf.at[h, :, rows_of(to), :],
            out.at[:, :, pl.ds(pl.multiple_of(ms * width + h * hd, hd), hd)],
            o_send.at[i, h],
            o_recv.at[ms, h],
            {"seq": to},
        )

    def o_local(h):
        return pltpu.make_async_copy(
            gbuf.at[h, :, rows_of(ms), :],
            out.at[:, :, pl.ds(pl.multiple_of(ms * width + h * hd, hd), hd)],
            o_send.at[0, h],
        )

    def head(h, carry):
        mine = pl.ds(pl.multiple_of(h * hd, hd), hd)

        def text_cols(j):
            return pl.ds(pl.multiple_of((h * 3 + j) * hd, hd), hd)

        def joint(j):
            return jnp.concatenate(
                [vbuf[j, :, mine].astype(F32), tfull[:, text_cols(j)]], axis=0
            )

        gq = gain_q[pl.ds(h, 1), :]
        gk = gain_k[pl.ds(h, 1), :]
        q = joint(0)
        k = joint(1)
        v = joint(2).astype(BF)
        qn_s[...] = (q * inverse(q) * gq).astype(BF)
        kn32 = (k * inverse(k) * gk).astype(BF).astype(F32)
        kn = kn32.astype(BF)
        kn_t = kn32.T.astype(BF)
        u_s[:tokens] = vbuf[3, :, mine]
        u_s[tokens:] = up_text[:, mine]

        def block(n, first):
            at = pl.ds(pl.multiple_of(n * blk, blk), blk)
            qb = qn_s[at, :]
            ub = u_s[at, :]
            e = jnp.exp2(dot_nt(kn, qb) * (scale * math.log2(math.e)))
            e = jnp.concatenate([e[:tokens], jnp.where(valid, e[tokens:], 0.0)], axis=0)
            probs = e * (1.0 / jnp.sum(e, axis=0, keepdims=True))
            grad_probs = dot_nt(v, ub)
            delta = jnp.sum(probs * grad_probs, axis=0, keepdims=True)
            grad_scores = (probs * (grad_probs - delta) * scale).astype(BF)
            dv = dot_nn(probs.astype(BF), ub)
            dk = dot_nn(grad_scores, qb)
            dq_s[at, :] = dot_nn(kn_t, grad_scores).T
            if first:
                dk_s[...] = dk
                dv_s[...] = dv
            else:
                dk_s[...] += dk
                dv_s[...] += dv

        block(0, True)
        if rows > blk:
            lax.fori_loop(1, rows // blk, lambda n, c: (block(n, False), c)[1], 0)
        grads = (
            norm_back(q, inverse(q), gq, dq_s[...]),
            norm_back(k, inverse(k), gk, dk_s[...]),
            dv_s[...],
        )
        for j in range(3):
            gbuf[h, j] = grads[j][:tokens].astype(BF)
            out_text[:, text_cols(j)] = grads[j][tokens:].astype(BF)
        for i in range(1, seq):
            o_copy(h, i).start()
        o_local(h).start()
        return carry

    lax.fori_loop(0, heads, head, 0)

    def finish(h, carry):
        o_local(h).wait()
        for i in range(1, seq):
            s = seq_peer(i)
            o_copy(h, i).wait_send()
            remote(
                gbuf.at[h, :, rows_of(s), :],
                out.at[:, :, pl.ds(pl.multiple_of(s * width + h * hd, hd), hd)],
                o_send.at[i, h],
                o_recv.at[s, h],
                {"seq": s},
            ).wait_recv()
        return carry

    lax.fori_loop(0, heads, finish, 0)

    def drain(n, carry):
        c = dp_peer(n)
        for i in range(1, seq):
            r_copy(c, i).wait_send()
        return carry

    lax.fori_loop(0, dp, drain, 0)
    for n in range(1, dp):
        z_copy(dp_peer(n)).wait_send()
    for i in range(1, half):
        x_copy(i).wait_send()
    for i in range(half):
        g = lax.rem(md + dp - 2 * i, dp)
        forward(g, xall.at[g]).wait_send()
    for i in range(1, seq):
        v_copy(i).wait_send()
        u_copy(i).wait_send()
        t_copy(i).wait_send()


def shards(
    seq,
    dp,
    video_qkv,
    video_cotangent,
    prompt_states,
    text_weight,
    text_cotangent,
    gain_query,
    gain_key,
    prompt_lengths,
    prompt_source,
):
    heads, hd = gain_query.shape
    tok = video_qkv.shape[1]
    every = video_qkv.shape[3]
    tokens = tok * seq
    prompt, feat = prompt_states.shape[1:]
    cols = text_weight.shape[1]
    part = prompt // seq
    per = dp // seq
    rows = tokens + prompt
    blk = rows if rows <= 640 else prompt
    width = heads * hd
    dma = pltpu.SemaphoreType.DMA
    hbm = pl.BlockSpec(memory_space=pl.ANY)
    vmem = pl.BlockSpec(memory_space=pltpu.VMEM)
    smem = pl.BlockSpec(memory_space=pltpu.SMEM)
    grad_video, grad_text = pl.pallas_call(
        functools.partial(kernel, seq, dp, blk),
        out_shape=(
            jax.ShapeDtypeStruct((3, tok, every), BF),
            jax.ShapeDtypeStruct((prompt, 3 * width), BF),
        ),
        in_specs=[hbm, hbm, vmem, hbm, vmem, vmem, vmem, smem, smem],
        out_specs=(hbm, vmem),
        scratch_shapes=[
            pltpu.VMEM((dp, prompt, feat), BF),
            pltpu.VMEM((feat, cols), BF),
            pltpu.VMEM((4, tokens, width), BF),
            pltpu.VMEM((seq, dp, part, cols), BF),
            pltpu.VMEM((seq, dp, part, cols), BF),
            pltpu.VMEM((dp, part, cols), BF),
            pltpu.VMEM((dp, part, cols), BF),
            pltpu.VMEM((seq, per, part, cols), BF),
            pltpu.VMEM((prompt, per * cols), F32),
            pltpu.VMEM((rows, hd), BF),
            pltpu.VMEM((rows, hd), BF),
            pltpu.VMEM((rows, hd), F32),
            pltpu.VMEM((rows, hd), F32),
            pltpu.VMEM((rows, hd), F32),
            pltpu.VMEM((heads, 3, tokens, hd), BF),
            dma((dp,)),
            dma((dp,)),
            dma((dp,)),
            dma((seq, 2)),
            dma((seq, 2)),
            dma((seq, dp)),
            dma((seq, dp)),
            dma((dp,)),
            dma((dp,)),
            dma((seq,)),
            dma((seq,)),
            dma((seq, heads)),
            dma((seq, heads)),
            dma((4,)),
        ],
        compiler_params=pltpu.CompilerParams(
            collective_id=0, has_side_effects=True, vmem_limit_bytes=56 * 1024 * 1024
        ),
    )(
        jnp.transpose(video_qkv[0], (1, 0, 2)),
        video_cotangent[0],
        prompt_states[0],
        text_weight,
        text_cotangent[0],
        gain_query,
        gain_key,
        prompt_lengths,
        prompt_source,
    )
    return jnp.transpose(grad_video, (1, 0, 2))[None], grad_text[None]


def solution(mesh):
    in_specs = (
        P("dp", "seq", None, None),
        P("dp", "seq", None),
        P("dp", None, "seq"),
        P("seq", "dp"),
        P("dp", None, "seq"),
        P("seq", None),
        P("seq", None),
        P("dp"),
        P(),
    )
    out_specs = (P("dp", "seq", None, None), P("dp", None, "seq"))
    body = functools.partial(shards, mesh.shape["seq"], mesh.shape["dp"])
    return jax.shard_map(body, mesh=mesh, in_specs=in_specs, out_specs=out_specs, check_vma=False)
```

```python
import functools
import math

import jax
import jax.numpy as jnp
from jax import lax
from jax.experimental import pallas as pl
from jax.experimental.pallas import tpu as pltpu
from jax.sharding import PartitionSpec as P

EPS = 1e-06
BF = jnp.bfloat16
F32 = jnp.float32


def dot_nt(a, b):
    return lax.dot_general(a, b, (((1,), (1,)), ((), ())), preferred_element_type=F32)


def dot_nn(a, b):
    return jnp.dot(a, b, preferred_element_type=F32)


def kernel(
    seq,
    dp,
    blk,
    qkv,
    cot,
    states,
    weight,
    up_text,
    gain_q,
    gain_k,
    length,
    source,
    out,
    out_text,
    xall,
    wbuf,
    vbuf,
    pbuf,
    rbuf,
    sums,
    zsend,
    tbuf,
    tfull,
    qn_s,
    u_s,
    dq_s,
    dk_s,
    dv_s,
    gbuf,
    up_send,
    down_send,
    f_send,
    x_recv,
    v_send,
    v_recv,
    u_send,
    u_recv,
    r_send,
    r_recv,
    z_send,
    t_recv,
    o_send,
    o_recv,
    l_sem,
):
    ms = lax.axis_index("seq")
    md = lax.axis_index("dp")
    heads = gain_q.shape[0]
    hd = gain_q.shape[1]
    tok = qkv.shape[1]
    tokens = seq * tok
    prompt = states.shape[0]
    part = prompt // seq
    cols = weight.shape[1]
    per = dp // seq
    width = heads * hd
    half = dp // 2
    partner = md + 1 - 2 * lax.rem(md, 2)

    def seq_peer(i):
        return lax.rem(ms + i, seq)

    def dp_peer(i):
        return lax.rem(md + i, dp)

    def remote(src, dst, send, recv, where):
        return pltpu.make_async_remote_copy(
            src_ref=src,
            dst_ref=dst,
            send_sem=send,
            recv_sem=recv,
            device_id=where,
            device_id_type=pl.DeviceIdType.MESH,
        )

    barrier = pltpu.get_barrier_semaphore()
    for i in range(1, seq):
        pl.semaphore_signal(
            barrier, inc=1, device_id={"seq": seq_peer(i)}, device_id_type=pl.DeviceIdType.MESH
        )
    for i in range(1, dp):
        pl.semaphore_signal(
            barrier, inc=1, device_id={"dp": dp_peer(i)}, device_id_type=pl.DeviceIdType.MESH
        )

    for i in range(seq):
        for k in range(per):
            @pl.when((seq_peer(i) != ms) | (ms * per + k != md))
            def _(i=i, k=k):
                pl.semaphore_signal(
                    barrier,
                    inc=1,
                    device_id={"seq": seq_peer(i), "dp": ms * per + k},
                    device_id_type=pl.DeviceIdType.MESH,
                )

    def rows_of(s):
        return pl.ds(pl.multiple_of(s * tok, tok), tok)

    def width_of(s):
        return pl.ds(pl.multiple_of(s * width, width), width)

    local_w = pltpu.make_async_copy(weight, wbuf, l_sem.at[1])
    local_w.start()
    pl.semaphore_wait(barrier, seq - 1 + dp - 1 + dp - jnp.where(md // per == ms, 1, 0))

    FIRST, SECOND = min(2, heads), min(3, heads)
    core = lax.rem(md, 2)
    place = md // 2

    def hop(g, src, up):
        return remote(
            src,
            xall.at[g],
            (up_send if up else down_send).at[g],
            x_recv.at[g],
            {"dp": md + 2 if up else md - 2},
        )

    def forward(g, src):
        return remote(src, xall.at[g], f_send.at[g], x_recv.at[g], {"dp": partner})

    def x_arrived(g):
        remote(states, xall.at[g], f_send.at[g], x_recv.at[g], {"dp": partner}).wait_recv()

    @pl.when(place + 1 < half)
    def _():
        hop(md, states, True).start()

    @pl.when(place > 0)
    def _():
        hop(md, states, False).start()

    forward(md, states).start()

    def head_cols(s, h):
        return pl.ds(pl.multiple_of(s * width + h * hd, hd), hd)

    def v_copy(h, i):
        to = seq_peer(i)
        return remote(
            qkv.at[:, :, head_cols(to, h)],
            vbuf.at[h, pl.ds(0, 3), rows_of(ms), :],
            v_send.at[i, h],
            v_recv.at[ms, h],
            {"seq": to},
        )

    def u_copy(h, i):
        to = seq_peer(i)
        return remote(
            cot.at[:, head_cols(to, h)],
            vbuf.at[h, 3, rows_of(ms), :],
            u_send.at[i, h],
            u_recv.at[ms, h],
            {"seq": to},
        )

    def send_head(h):
        for i in range(1, seq):
            v_copy(h, i).start()
            u_copy(h, i).start()

    def own_qkv(h):
        return pltpu.make_async_copy(
            qkv.at[:, :, head_cols(ms, h)],
            vbuf.at[h, pl.ds(0, 3), rows_of(ms), :],
            v_send.at[0, h],
        )

    def own_cot(h):
        return pltpu.make_async_copy(
            cot.at[:, head_cols(ms, h)], vbuf.at[h, 3, rows_of(ms), :], u_send.at[0, h]
        )

    def head_arrived(h):
        own_qkv(h).wait()
        own_cot(h).wait()
        for i in range(1, seq):
            s = seq_peer(i)
            remote(
                qkv.at[:, :, head_cols(s, h)],
                vbuf.at[h, pl.ds(0, 3), rows_of(s), :],
                v_send.at[i, h],
                v_recv.at[s, h],
                {"seq": s},
            ).wait_recv()
            remote(
                cot.at[:, head_cols(s, h)],
                vbuf.at[h, 3, rows_of(s), :],
                u_send.at[i, h],
                u_recv.at[s, h],
                {"seq": s},
            ).wait_recv()

    def r_copy(g, i):
        to = seq_peer(i)
        return remote(
            pbuf.at[to, g], rbuf.at[ms, g], r_send.at[i, g], r_recv.at[ms, g], {"seq": to}
        )

    def project(g, value):
        value = dot_nn(value, wbuf[...])
        for q in range(seq):
            pbuf[q, g] = value[q * part : (q + 1) * part].astype(BF)
        for i in range(1, seq):
            r_copy(g, i).start()

    local_w.wait()
    project(md, states[...])
    x_arrived(partner)
    project(partner, xall[partner])
    for h in range(FIRST):
        send_head(h)

    def step(k, carry):
        low = place - k
        high = place + k

        @pl.when(low >= 0)
        def _():
            g = 2 * low + core
            x_arrived(g)

            @pl.when(place + 1 < half)
            def _():
                hop(g, xall.at[g], True).start()

            forward(g, xall.at[g]).start()

        @pl.when(high < half)
        def _():
            g = 2 * high + core
            x_arrived(g)

            @pl.when(place > 0)
            def _():
                hop(g, xall.at[g], False).start()

            forward(g, xall.at[g]).start()

        @pl.when(low >= 0)
        def _():
            g = 2 * low + core
            project(g, xall[g])
            x_arrived(2 * low + 1 - core)
            project(2 * low + 1 - core, xall[2 * low + 1 - core])

        @pl.when(high < half)
        def _():
            g = 2 * high + core
            project(g, xall[g])
            x_arrived(2 * high + 1 - core)
            project(2 * high + 1 - core, xall[2 * high + 1 - core])

        return carry

    lax.fori_loop(1, half, step, 0)
    for h in range(FIRST, SECOND):
        send_head(h)

    def reduce_step(g, carry):
        total = pbuf[ms, g].astype(F32)
        for i in range(1, seq):
            s = seq_peer(i)
            remote(
                pbuf.at[s, g], rbuf.at[s, g], r_send.at[i, g], r_recv.at[s, g], {"seq": s}
            ).wait_recv()
            total = total + rbuf[s, g].astype(F32)
        sums[g] = total.astype(BF)
        return carry

    lax.fori_loop(0, dp, reduce_step, 0)

    goal = md // per
    slot = lax.rem(md, per)

    def z_copy(c):
        return remote(
            zsend.at[c], tbuf.at[ms, slot], z_send.at[c], t_recv.at[ms, slot], {"seq": goal, "dp": c}
        )

    def z_step(n, carry):
        c = dp_peer(n)
        zsend[c] = sums[source[c]]
        z_copy(c).start()
        return carry

    lax.fori_loop(1, dp, z_step, 0)
    zsend[md] = sums[source[md]]

    @pl.when(goal == ms)
    def _():
        tbuf[ms, slot] = zsend[md]

    @pl.when(goal != ms)
    def _():
        z_copy(md).start()

    for h in range(SECOND, heads):
        send_head(h)
    for h in range(heads):
        own_qkv(h).start()
        own_cot(h).start()

    def t_arrived(s, k):
        @pl.when((s != ms) | (ms * per + k != md))
        def _():
            remote(
                zsend.at[0], tbuf.at[s, k], z_send.at[0], t_recv.at[s, k], {"seq": seq_peer(1)}
            ).wait_recv()

    for s in range(seq):
        for k in range(per):
            t_arrived(s, k)
    for s in range(seq):
        for k in range(per):
            tfull[s * part : (s + 1) * part, k * cols : (k + 1) * cols] = tbuf[s, k].astype(F32)

    rows = tokens + prompt
    scale = 1.0 / math.sqrt(hd)
    valid = lax.broadcasted_iota(jnp.int32, (prompt, blk), 0) < length[0]

    def inverse(x):
        return lax.rsqrt(jnp.mean(x * x, axis=-1, keepdims=True) + EPS)

    def norm_back(x, r, gain, grad):
        scaled = grad * gain
        inner = jnp.mean(scaled * x, axis=-1, keepdims=True)
        return r * scaled - x * (r * r * r * inner)

    def o_copy(h, i):
        to = seq_peer(i)
        return remote(
            gbuf.at[h, :, rows_of(to), :],
            out.at[:, :, pl.ds(pl.multiple_of(ms * width + h * hd, hd), hd)],
            o_send.at[i, h],
            o_recv.at[ms, h],
            {"seq": to},
        )

    def o_local(h):
        return pltpu.make_async_copy(
            gbuf.at[h, :, rows_of(ms), :],
            out.at[:, :, pl.ds(pl.multiple_of(ms * width + h * hd, hd), hd)],
            o_send.at[0, h],
        )

    def head(h, carry):
        mine = pl.ds(pl.multiple_of(h * hd, hd), hd)

        def text_cols(j):
            return pl.ds(pl.multiple_of((h * 3 + j) * hd, hd), hd)

        def joint(j):
            return jnp.concatenate(
                [vbuf[h, j].astype(F32), tfull[:, text_cols(j)]], axis=0
            )

        head_arrived(h)
        gq = gain_q[pl.ds(h, 1), :]
        gk = gain_k[pl.ds(h, 1), :]
        q = joint(0)
        k = joint(1)
        v = joint(2).astype(BF)
        qn_s[...] = (q * inverse(q) * gq).astype(BF)
        kn32 = (k * inverse(k) * gk).astype(BF).astype(F32)
        kn = kn32.astype(BF)
        kn_t = kn32.T.astype(BF)
        u_s[:tokens] = vbuf[h, 3]
        u_s[tokens:] = up_text[:, mine]

        def block(n, first):
            at = pl.ds(pl.multiple_of(n * blk, blk), blk)
            qb = qn_s[at, :]
            ub = u_s[at, :]
            e = jnp.exp2(dot_nt(kn, qb) * (scale * math.log2(math.e)))
            e = jnp.concatenate([e[:tokens], jnp.where(valid, e[tokens:], 0.0)], axis=0)
            probs = e * (1.0 / jnp.sum(e, axis=0, keepdims=True))
            grad_probs = dot_nt(v, ub)
            delta = jnp.sum(probs * grad_probs, axis=0, keepdims=True)
            grad_scores = (probs * (grad_probs - delta) * scale).astype(BF)
            dv = dot_nn(probs.astype(BF), ub)
            dk = dot_nn(grad_scores, qb)
            dq_s[at, :] = dot_nn(kn_t, grad_scores).T
            if first:
                dk_s[...] = dk
                dv_s[...] = dv
            else:
                dk_s[...] += dk
                dv_s[...] += dv

        block(0, True)
        if rows > blk:
            lax.fori_loop(1, rows // blk, lambda n, c: (block(n, False), c)[1], 0)
        grads = (
            norm_back(q, inverse(q), gq, dq_s[...]),
            norm_back(k, inverse(k), gk, dk_s[...]),
            dv_s[...],
        )
        for j in range(3):
            gbuf[h, j] = grads[j][:tokens].astype(BF)
            out_text[:, text_cols(j)] = grads[j][tokens:].astype(BF)
        for i in range(1, seq):
            o_copy(h, i).start()
        o_local(h).start()
        return carry

    lax.fori_loop(0, heads, head, 0)

    def finish(h, carry):
        o_local(h).wait()
        for i in range(1, seq):
            s = seq_peer(i)
            o_copy(h, i).wait_send()
            remote(
                gbuf.at[h, :, rows_of(s), :],
                out.at[:, :, pl.ds(pl.multiple_of(s * width + h * hd, hd), hd)],
                o_send.at[i, h],
                o_recv.at[s, h],
                {"seq": s},
            ).wait_recv()
        return carry

    lax.fori_loop(0, heads, finish, 0)

    def forward_wait(g):
        @pl.when(lax.rem(g, 2) == core)
        def _():
            forward(g, xall.at[g]).wait_send()
            at = g // 2

            @pl.when((at <= place) & (place + 1 < half))
            def _():
                hop(g, xall.at[g], True).wait_send()

            @pl.when((at >= place) & (place > 0))
            def _():
                hop(g, xall.at[g], False).wait_send()

    def drain(n, carry):
        for i in range(1, seq):
            r_copy(n, i).wait_send()
        forward_wait(n)
        return carry

    lax.fori_loop(0, dp, drain, 0)
    for n in range(1, dp):
        z_copy(dp_peer(n)).wait_send()

    @pl.when(goal != ms)
    def _():
        z_copy(md).wait_send()

    for i in range(1, seq):
        for h in range(heads):
            v_copy(h, i).wait_send()
            u_copy(h, i).wait_send()


def shards(
    seq,
    dp,
    video_qkv,
    video_cotangent,
    prompt_states,
    text_weight,
    text_cotangent,
    gain_query,
    gain_key,
    prompt_lengths,
    prompt_source,
):
    heads, hd = gain_query.shape
    tok = video_qkv.shape[1]
    every = video_qkv.shape[3]
    tokens = tok * seq
    prompt, feat = prompt_states.shape[1:]
    cols = text_weight.shape[1]
    part = prompt // seq
    per = dp // seq
    rows = tokens + prompt
    blk = rows if rows <= 640 else prompt
    width = heads * hd
    dma = pltpu.SemaphoreType.DMA
    hbm = pl.BlockSpec(memory_space=pl.ANY)
    vmem = pl.BlockSpec(memory_space=pltpu.VMEM)
    smem = pl.BlockSpec(memory_space=pltpu.SMEM)
    grad_video, grad_text = pl.pallas_call(
        functools.partial(kernel, seq, dp, blk),
        out_shape=(
            jax.ShapeDtypeStruct((3, tok, every), BF),
            jax.ShapeDtypeStruct((prompt, 3 * width), BF),
        ),
        in_specs=[hbm, hbm, vmem, hbm, vmem, vmem, vmem, smem, smem],
        out_specs=(hbm, vmem),
        scratch_shapes=[
            pltpu.VMEM((dp, prompt, feat), BF),
            pltpu.VMEM((feat, cols), BF),
            pltpu.VMEM((heads, 4, tokens, hd), BF),
            pltpu.VMEM((seq, dp, part, cols), BF),
            pltpu.VMEM((seq, dp, part, cols), BF),
            pltpu.VMEM((dp, part, cols), BF),
            pltpu.VMEM((dp, part, cols), BF),
            pltpu.VMEM((seq, per, part, cols), BF),
            pltpu.VMEM((prompt, per * cols), F32),
            pltpu.VMEM((rows, hd), BF),
            pltpu.VMEM((rows, hd), BF),
            pltpu.VMEM((rows, hd), F32),
            pltpu.VMEM((rows, hd), F32),
            pltpu.VMEM((rows, hd), F32),
            pltpu.VMEM((heads, 3, tokens, hd), BF),
            dma((dp,)),
            dma((dp,)),
            dma((dp,)),
            dma((dp,)),
            dma((seq, heads)),
            dma((seq, heads)),
            dma((seq, heads)),
            dma((seq, heads)),
            dma((seq, dp)),
            dma((seq, dp)),
            dma((dp,)),
            dma((seq, per)),
            dma((seq, heads)),
            dma((seq, heads)),
            dma((4,)),
        ],
        compiler_params=pltpu.CompilerParams(
            collective_id=0, has_side_effects=True, vmem_limit_bytes=56 * 1024 * 1024
        ),
    )(
        jnp.transpose(video_qkv[0], (1, 0, 2)),
        video_cotangent[0],
        prompt_states[0],
        text_weight,
        text_cotangent[0],
        gain_query,
        gain_key,
        prompt_lengths,
        prompt_source,
    )
    return jnp.transpose(grad_video, (1, 0, 2))[None], grad_text[None]


def solution(mesh):
    in_specs = (
        P("dp", "seq", None, None),
        P("dp", "seq", None),
        P("dp", None, "seq"),
        P("seq", "dp"),
        P("dp", None, "seq"),
        P("seq", None),
        P("seq", None),
        P("dp"),
        P(),
    )
    out_specs = (P("dp", "seq", None, None), P("dp", None, "seq"))
    body = functools.partial(shards, mesh.shape["seq"], mesh.shape["dp"])
    return jax.shard_map(body, mesh=mesh, in_specs=in_specs, out_specs=out_specs, check_vma=False)
```

```python
import functools
import math

import jax
import jax.numpy as jnp
from jax import lax
from jax.experimental import pallas as pl
from jax.experimental.pallas import tpu as pltpu
from jax.sharding import PartitionSpec as P

EPS = 1e-06
BF = jnp.bfloat16
F32 = jnp.float32


def dot_nt(a, b):
    return lax.dot_general(a, b, (((1,), (1,)), ((), ())), preferred_element_type=F32)


def dot_nn(a, b):
    return jnp.dot(a, b, preferred_element_type=F32)


def kernel(
    seq,
    dp,
    blk,
    qkv,
    cot,
    states,
    weight,
    up_text,
    gain_q,
    gain_k,
    length,
    source,
    out,
    out_text,
    xall,
    wbuf,
    vbuf,
    pbuf,
    rbuf,
    sums,
    zsend,
    tbuf,
    tfull,
    qn_s,
    u_s,
    dq_s,
    dk_s,
    dv_s,
    gbuf,
    up_s,
    text_s,
    up_send,
    down_send,
    f_send,
    x_recv,
    v_send,
    v_recv,
    u_send,
    u_recv,
    r_send,
    r_recv,
    z_send,
    t_recv,
    o_send,
    o_recv,
    l_sem,
    text_sem,
):
    ms = lax.axis_index("seq")
    md = lax.axis_index("dp")
    heads = gain_q.shape[0]
    hd = gain_q.shape[1]
    tok = qkv.shape[1]
    tokens = seq * tok
    prompt = states.shape[0]
    part = prompt // seq
    cols = weight.shape[1]
    per = dp // seq
    width = heads * hd
    half = dp // 2
    partner = md + 1 - 2 * lax.rem(md, 2)

    def seq_peer(i):
        return lax.rem(ms + i, seq)

    def dp_peer(i):
        return lax.rem(md + i, dp)

    def remote(src, dst, send, recv, where):
        return pltpu.make_async_remote_copy(
            src_ref=src,
            dst_ref=dst,
            send_sem=send,
            recv_sem=recv,
            device_id=where,
            device_id_type=pl.DeviceIdType.MESH,
        )

    barrier = pltpu.get_barrier_semaphore()
    for i in range(1, seq):
        pl.semaphore_signal(
            barrier, inc=1, device_id={"seq": seq_peer(i)}, device_id_type=pl.DeviceIdType.MESH
        )
    for i in range(1, dp):
        pl.semaphore_signal(
            barrier, inc=1, device_id={"dp": dp_peer(i)}, device_id_type=pl.DeviceIdType.MESH
        )

    for i in range(seq):
        for k in range(per):
            @pl.when((seq_peer(i) != ms) | (ms * per + k != md))
            def _(i=i, k=k):
                pl.semaphore_signal(
                    barrier,
                    inc=1,
                    device_id={"seq": seq_peer(i), "dp": ms * per + k},
                    device_id_type=pl.DeviceIdType.MESH,
                )

    def rows_of(s):
        return pl.ds(pl.multiple_of(s * tok, tok), tok)

    def width_of(s):
        return pl.ds(pl.multiple_of(s * width, width), width)

    local_w = pltpu.make_async_copy(weight, wbuf, l_sem.at[1])
    local_x = pltpu.make_async_copy(states, xall.at[md], l_sem.at[0])
    local_u = pltpu.make_async_copy(up_text, up_s, l_sem.at[2])
    local_x.start()
    local_w.start()
    local_u.start()
    pl.semaphore_wait(barrier, seq - 1 + dp - 1 + dp - jnp.where(md // per == ms, 1, 0))

    FIRST, SECOND = min(2, heads), min(3, heads)
    core = lax.rem(md, 2)
    place = md // 2

    def hop(g, src, up):
        return remote(
            src,
            xall.at[g],
            (up_send if up else down_send).at[g],
            x_recv.at[g],
            {"dp": md + 2 if up else md - 2},
        )

    def forward(g, src):
        return remote(src, xall.at[g], f_send.at[g], x_recv.at[g], {"dp": partner})

    def x_arrived(g):
        remote(states, xall.at[g], f_send.at[g], x_recv.at[g], {"dp": partner}).wait_recv()

    @pl.when(place + 1 < half)
    def _():
        hop(md, states, True).start()

    @pl.when(place > 0)
    def _():
        hop(md, states, False).start()

    forward(md, states).start()

    def head_cols(s, h):
        return pl.ds(pl.multiple_of(s * width + h * hd, hd), hd)

    def v_copy(h, i):
        to = seq_peer(i)
        return remote(
            qkv.at[:, :, head_cols(to, h)],
            vbuf.at[h, pl.ds(0, 3), rows_of(ms), :],
            v_send.at[i, h],
            v_recv.at[ms, h],
            {"seq": to},
        )

    def u_copy(h, i):
        to = seq_peer(i)
        return remote(
            cot.at[:, head_cols(to, h)],
            vbuf.at[h, 3, rows_of(ms), :],
            u_send.at[i, h],
            u_recv.at[ms, h],
            {"seq": to},
        )

    def send_head(h):
        for i in range(1, seq):
            v_copy(h, i).start()
            u_copy(h, i).start()

    def own_qkv(h):
        return pltpu.make_async_copy(
            qkv.at[:, :, head_cols(ms, h)],
            vbuf.at[h, pl.ds(0, 3), rows_of(ms), :],
            v_send.at[0, h],
        )

    def own_cot(h):
        return pltpu.make_async_copy(
            cot.at[:, head_cols(ms, h)], vbuf.at[h, 3, rows_of(ms), :], u_send.at[0, h]
        )

    def head_arrived(h):
        own_qkv(h).wait()
        own_cot(h).wait()
        for i in range(1, seq):
            s = seq_peer(i)
            remote(
                qkv.at[:, :, head_cols(s, h)],
                vbuf.at[h, pl.ds(0, 3), rows_of(s), :],
                v_send.at[i, h],
                v_recv.at[s, h],
                {"seq": s},
            ).wait_recv()
            remote(
                cot.at[:, head_cols(s, h)],
                vbuf.at[h, 3, rows_of(s), :],
                u_send.at[i, h],
                u_recv.at[s, h],
                {"seq": s},
            ).wait_recv()

    def r_copy(g, i):
        to = seq_peer(i)
        return remote(
            pbuf.at[to, g], rbuf.at[ms, g], r_send.at[i, g], r_recv.at[ms, g], {"seq": to}
        )

    def project(g, value):
        value = dot_nn(value, wbuf[...])
        for q in range(seq):
            pbuf[q, g] = value[q * part : (q + 1) * part].astype(BF)
        for i in range(1, seq):
            r_copy(g, i).start()

    local_x.wait()
    local_w.wait()
    project(md, xall[md])
    x_arrived(partner)
    project(partner, xall[partner])
    for h in range(FIRST):
        send_head(h)

    def step(k, carry):
        low = place - k
        high = place + k

        @pl.when(low >= 0)
        def _():
            g = 2 * low + core
            x_arrived(g)

            @pl.when(place + 1 < half)
            def _():
                hop(g, xall.at[g], True).start()

            forward(g, xall.at[g]).start()

        @pl.when(high < half)
        def _():
            g = 2 * high + core
            x_arrived(g)

            @pl.when(place > 0)
            def _():
                hop(g, xall.at[g], False).start()

            forward(g, xall.at[g]).start()

        @pl.when(low >= 0)
        def _():
            g = 2 * low + core
            project(g, xall[g])
            x_arrived(2 * low + 1 - core)
            project(2 * low + 1 - core, xall[2 * low + 1 - core])

        @pl.when(high < half)
        def _():
            g = 2 * high + core
            project(g, xall[g])
            x_arrived(2 * high + 1 - core)
            project(2 * high + 1 - core, xall[2 * high + 1 - core])

        return carry

    lax.fori_loop(1, half, step, 0)
    for h in range(FIRST, SECOND):
        send_head(h)

    def reduce_step(g, carry):
        total = pbuf[ms, g].astype(F32)
        for i in range(1, seq):
            s = seq_peer(i)
            remote(
                pbuf.at[s, g], rbuf.at[s, g], r_send.at[i, g], r_recv.at[s, g], {"seq": s}
            ).wait_recv()
            total = total + rbuf[s, g].astype(F32)
        sums[g] = total.astype(BF)
        return carry

    lax.fori_loop(0, dp, reduce_step, 0)

    goal = md // per
    slot = lax.rem(md, per)

    def z_copy(c):
        return remote(
            zsend.at[c], tbuf.at[ms, slot], z_send.at[c], t_recv.at[ms, slot], {"seq": goal, "dp": c}
        )

    def z_step(n, carry):
        c = dp_peer(n)
        zsend[c] = sums[source[c]]
        z_copy(c).start()
        return carry

    lax.fori_loop(1, dp, z_step, 0)
    zsend[md] = sums[source[md]]

    @pl.when(goal == ms)
    def _():
        tbuf[ms, slot] = zsend[md]

    @pl.when(goal != ms)
    def _():
        z_copy(md).start()

    for h in range(SECOND, heads):
        send_head(h)
    for h in range(heads):
        own_qkv(h).start()
        own_cot(h).start()

    def t_arrived(s, k):
        @pl.when((s != ms) | (ms * per + k != md))
        def _():
            remote(
                zsend.at[0], tbuf.at[s, k], z_send.at[0], t_recv.at[s, k], {"seq": seq_peer(1)}
            ).wait_recv()

    for s in range(seq):
        for k in range(per):
            t_arrived(s, k)
    for s in range(seq):
        for k in range(per):
            tfull[s * part : (s + 1) * part, k * cols : (k + 1) * cols] = tbuf[s, k].astype(F32)

    rows = tokens + prompt
    scale = 1.0 / math.sqrt(hd)
    valid = lax.broadcasted_iota(jnp.int32, (prompt, blk), 0) < length[0]

    def inverse(x):
        return lax.rsqrt(jnp.mean(x * x, axis=-1, keepdims=True) + EPS)

    def norm_back(x, r, gain, grad):
        scaled = grad * gain
        inner = jnp.mean(scaled * x, axis=-1, keepdims=True)
        return r * scaled - x * (r * r * r * inner)

    def o_copy(h, i):
        to = seq_peer(i)
        return remote(
            gbuf.at[h, :, rows_of(to), :],
            out.at[:, :, pl.ds(pl.multiple_of(ms * width + h * hd, hd), hd)],
            o_send.at[i, h],
            o_recv.at[ms, h],
            {"seq": to},
        )

    def o_local(h):
        return pltpu.make_async_copy(
            gbuf.at[h, :, rows_of(ms), :],
            out.at[:, :, pl.ds(pl.multiple_of(ms * width + h * hd, hd), hd)],
            o_send.at[0, h],
        )

    def text_local(h):
        at = pl.ds(pl.multiple_of(h * 3 * hd, 3 * hd), 3 * hd)
        return pltpu.make_async_copy(text_s.at[:, at], out_text.at[:, at], text_sem.at[h])

    def head(h, carry):
        mine = pl.ds(pl.multiple_of(h * hd, hd), hd)

        def text_cols(j):
            return pl.ds(pl.multiple_of((h * 3 + j) * hd, hd), hd)

        def joint(j):
            return jnp.concatenate(
                [vbuf[h, j].astype(F32), tfull[:, text_cols(j)]], axis=0
            )

        head_arrived(h)
        gq = gain_q[pl.ds(h, 1), :]
        gk = gain_k[pl.ds(h, 1), :]
        q = joint(0)
        k = joint(1)
        v = joint(2).astype(BF)
        qn_s[...] = (q * inverse(q) * gq).astype(BF)
        kn32 = (k * inverse(k) * gk).astype(BF).astype(F32)
        kn = kn32.astype(BF)
        kn_t = kn32.T.astype(BF)
        u_s[:tokens] = vbuf[h, 3]
        u_s[tokens:] = up_s[:, mine]

        def block(n, first):
            at = pl.ds(pl.multiple_of(n * blk, blk), blk)
            qb = qn_s[at, :]
            ub = u_s[at, :]
            e = jnp.exp2(dot_nt(kn, qb) * (scale * math.log2(math.e)))
            e = jnp.concatenate([e[:tokens], jnp.where(valid, e[tokens:], 0.0)], axis=0)
            probs = e * (1.0 / jnp.sum(e, axis=0, keepdims=True))
            grad_probs = dot_nt(v, ub)
            delta = jnp.sum(probs * grad_probs, axis=0, keepdims=True)
            grad_scores = (probs * (grad_probs - delta) * scale).astype(BF)
            dv = dot_nn(probs.astype(BF), ub)
            dk = dot_nn(grad_scores, qb)
            dq_s[at, :] = dot_nn(kn_t, grad_scores).T
            if first:
                dk_s[...] = dk
                dv_s[...] = dv
            else:
                dk_s[...] += dk
                dv_s[...] += dv

        block(0, True)
        if rows > blk:
            lax.fori_loop(1, rows // blk, lambda n, c: (block(n, False), c)[1], 0)
        grads = (
            norm_back(q, inverse(q), gq, dq_s[...]),
            norm_back(k, inverse(k), gk, dk_s[...]),
            dv_s[...],
        )
        for j in range(3):
            gbuf[h, j] = grads[j][:tokens].astype(BF)
            text_s[:, text_cols(j)] = grads[j][tokens:].astype(BF)
        for i in range(1, seq):
            o_copy(h, i).start()
        o_local(h).start()
        text_local(h).start()
        return carry

    local_u.wait()
    lax.fori_loop(0, heads, head, 0)

    def finish(h, carry):
        o_local(h).wait()
        text_local(h).wait()
        for i in range(1, seq):
            s = seq_peer(i)
            o_copy(h, i).wait_send()
            remote(
                gbuf.at[h, :, rows_of(s), :],
                out.at[:, :, pl.ds(pl.multiple_of(s * width + h * hd, hd), hd)],
                o_send.at[i, h],
                o_recv.at[s, h],
                {"seq": s},
            ).wait_recv()
        return carry

    lax.fori_loop(0, heads, finish, 0)

    def forward_wait(g):
        @pl.when(lax.rem(g, 2) == core)
        def _():
            forward(g, xall.at[g]).wait_send()
            at = g // 2

            @pl.when((at <= place) & (place + 1 < half))
            def _():
                hop(g, xall.at[g], True).wait_send()

            @pl.when((at >= place) & (place > 0))
            def _():
                hop(g, xall.at[g], False).wait_send()

    def drain(n, carry):
        for i in range(1, seq):
            r_copy(n, i).wait_send()
        forward_wait(n)
        return carry

    lax.fori_loop(0, dp, drain, 0)
    for n in range(1, dp):
        z_copy(dp_peer(n)).wait_send()

    @pl.when(goal != ms)
    def _():
        z_copy(md).wait_send()

    for i in range(1, seq):
        for h in range(heads):
            v_copy(h, i).wait_send()
            u_copy(h, i).wait_send()


def hand_over(video, text, video_out, text_out, sems):
    moves = [
        pltpu.make_async_copy(video.at[j], video_out.at[j], sems.at[j]) for j in range(3)
    ] + [pltpu.make_async_copy(text, text_out, sems.at[3])]
    for move in moves:
        move.start()
    for move in moves:
        move.wait()


def shards(
    seq,
    dp,
    video_qkv,
    video_cotangent,
    prompt_states,
    text_weight,
    text_cotangent,
    gain_query,
    gain_key,
    prompt_lengths,
    prompt_source,
):
    heads, hd = gain_query.shape
    tok = video_qkv.shape[1]
    every = video_qkv.shape[3]
    tokens = tok * seq
    prompt, feat = prompt_states.shape[1:]
    cols = text_weight.shape[1]
    part = prompt // seq
    per = dp // seq
    rows = tokens + prompt
    blk = rows if rows <= 640 else prompt
    width = heads * hd
    dma = pltpu.SemaphoreType.DMA
    hbm = pl.BlockSpec(memory_space=pl.ANY)
    vmem = pl.BlockSpec(memory_space=pltpu.VMEM)
    smem = pl.BlockSpec(memory_space=pltpu.SMEM)
    grad_video, grad_text = pl.pallas_call(
        functools.partial(kernel, seq, dp, blk),
        out_shape=(
            jax.ShapeDtypeStruct((3, tok, every), BF),
            jax.ShapeDtypeStruct((prompt, 3 * width), BF),
        ),
        in_specs=[hbm, hbm, hbm, hbm, hbm, vmem, vmem, smem, smem],
        out_specs=(hbm, hbm),
        scratch_shapes=[
            pltpu.VMEM((dp, prompt, feat), BF),
            pltpu.VMEM((feat, cols), BF),
            pltpu.VMEM((heads, 4, tokens, hd), BF),
            pltpu.VMEM((seq, dp, part, cols), BF),
            pltpu.VMEM((seq, dp, part, cols), BF),
            pltpu.VMEM((dp, part, cols), BF),
            pltpu.VMEM((dp, part, cols), BF),
            pltpu.VMEM((seq, per, part, cols), BF),
            pltpu.VMEM((prompt, per * cols), F32),
            pltpu.VMEM((rows, hd), BF),
            pltpu.VMEM((rows, hd), BF),
            pltpu.VMEM((rows, hd), F32),
            pltpu.VMEM((rows, hd), F32),
            pltpu.VMEM((rows, hd), F32),
            pltpu.VMEM((heads, 3, tokens, hd), BF),
            pltpu.VMEM((prompt, width), BF),
            pltpu.VMEM((prompt, 3 * width), BF),
            dma((dp,)),
            dma((dp,)),
            dma((dp,)),
            dma((dp,)),
            dma((seq, heads)),
            dma((seq, heads)),
            dma((seq, heads)),
            dma((seq, heads)),
            dma((seq, dp)),
            dma((seq, dp)),
            dma((dp,)),
            dma((seq, per)),
            dma((seq, heads)),
            dma((seq, heads)),
            dma((4,)),
            dma((heads,)),
        ],
        compiler_params=pltpu.CompilerParams(
            collective_id=0, has_side_effects=True, vmem_limit_bytes=56 * 1024 * 1024
        ),
    )(
        jnp.transpose(video_qkv[0], (1, 0, 2)),
        video_cotangent[0],
        prompt_states[0],
        text_weight,
        text_cotangent[0],
        gain_query,
        gain_key,
        prompt_lengths,
        prompt_source,
    )
    grad_video, grad_text = pl.pallas_call(
        hand_over,
        out_shape=(
            jax.ShapeDtypeStruct(grad_video.shape, BF),
            jax.ShapeDtypeStruct(grad_text.shape, BF),
        ),
        in_specs=[vmem, vmem],
        out_specs=(hbm, hbm),
        scratch_shapes=[dma((4,))],
    )(grad_video, grad_text)
    return jnp.transpose(grad_video, (1, 0, 2))[None], grad_text[None]


def solution(mesh):
    in_specs = (
        P("dp", "seq", None, None),
        P("dp", "seq", None),
        P("dp", None, "seq"),
        P("seq", "dp"),
        P("dp", None, "seq"),
        P("seq", None),
        P("seq", None),
        P("dp"),
        P(),
    )
    out_specs = (P("dp", "seq", None, None), P("dp", None, "seq"))
    body = functools.partial(shards, mesh.shape["seq"], mesh.shape["dp"])
    return jax.shard_map(body, mesh=mesh, in_specs=in_specs, out_specs=out_specs, check_vma=False)
```

```python
import functools
import math

import jax
import jax.numpy as jnp
from jax import lax
from jax.experimental import pallas as pl
from jax.experimental.pallas import tpu as pltpu
from jax.sharding import PartitionSpec as P

EPS = 1e-06
BF = jnp.bfloat16
F32 = jnp.float32


def dot_nt(a, b):
    return lax.dot_general(a, b, (((1,), (1,)), ((), ())), preferred_element_type=F32)


def dot_nn(a, b):
    return jnp.dot(a, b, preferred_element_type=F32)


def kernel(
    seq,
    dp,
    blk,
    qkv,
    cot,
    states,
    weight,
    up_text,
    gain_q,
    gain_k,
    length,
    source,
    out,
    out_text,
    xall,
    wbuf,
    vbuf,
    pbuf,
    rbuf,
    sums,
    zsend,
    tbuf,
    tfull,
    qn_s,
    u_s,
    dq_s,
    dk_s,
    dv_s,
    gbuf,
    up_s,
    text_s,
    up_send,
    down_send,
    f_send,
    x_recv,
    v_send,
    v_recv,
    u_send,
    u_recv,
    r_send,
    r_recv,
    z_send,
    t_recv,
    o_send,
    o_recv,
    l_sem,
    text_sem,
):
    ms = lax.axis_index("seq")
    md = lax.axis_index("dp")
    heads = gain_q.shape[0]
    hd = gain_q.shape[1]
    tok = qkv.shape[1]
    tokens = seq * tok
    prompt = states.shape[0]
    part = prompt // seq
    cols = weight.shape[1]
    per = dp // seq
    width = heads * hd
    half = dp // 2
    partner = md + 1 - 2 * lax.rem(md, 2)

    def seq_peer(i):
        return lax.rem(ms + i, seq)

    def dp_peer(i):
        return lax.rem(md + i, dp)

    def remote(src, dst, send, recv, where):
        return pltpu.make_async_remote_copy(
            src_ref=src,
            dst_ref=dst,
            send_sem=send,
            recv_sem=recv,
            device_id=where,
            device_id_type=pl.DeviceIdType.MESH,
        )

    barrier = pltpu.get_barrier_semaphore()
    for i in range(1, seq):
        pl.semaphore_signal(
            barrier, inc=1, device_id={"seq": seq_peer(i)}, device_id_type=pl.DeviceIdType.MESH
        )
    for i in range(1, dp):
        pl.semaphore_signal(
            barrier, inc=1, device_id={"dp": dp_peer(i)}, device_id_type=pl.DeviceIdType.MESH
        )

    for i in range(seq):
        for k in range(per):
            @pl.when((seq_peer(i) != ms) | (ms * per + k != md))
            def _(i=i, k=k):
                pl.semaphore_signal(
                    barrier,
                    inc=1,
                    device_id={"seq": seq_peer(i), "dp": ms * per + k},
                    device_id_type=pl.DeviceIdType.MESH,
                )

    def rows_of(s):
        return pl.ds(pl.multiple_of(s * tok, tok), tok)

    def width_of(s):
        return pl.ds(pl.multiple_of(s * width, width), width)

    local_w = pltpu.make_async_copy(weight, wbuf, l_sem.at[1])
    local_x = pltpu.make_async_copy(states, xall.at[md], l_sem.at[0])
    local_u = pltpu.make_async_copy(up_text, up_s, l_sem.at[2])
    local_x.start()
    local_w.start()
    local_u.start()
    pl.semaphore_wait(barrier, seq - 1 + dp - 1 + dp - jnp.where(md // per == ms, 1, 0))

    FIRST, SECOND = min(2, heads), min(3, heads)
    core = lax.rem(md, 2)
    place = md // 2

    def hop(g, src, up):
        return remote(
            src,
            xall.at[g],
            (up_send if up else down_send).at[g],
            x_recv.at[g],
            {"dp": md + 2 if up else md - 2},
        )

    def forward(g, src):
        return remote(src, xall.at[g], f_send.at[g], x_recv.at[g], {"dp": partner})

    def x_arrived(g):
        remote(states, xall.at[g], f_send.at[g], x_recv.at[g], {"dp": partner}).wait_recv()

    @pl.when(place + 1 < half)
    def _():
        hop(md, states, True).start()

    @pl.when(place > 0)
    def _():
        hop(md, states, False).start()

    forward(md, states).start()

    def head_cols(s, h):
        return pl.ds(pl.multiple_of(s * width + h * hd, hd), hd)

    def v_copy(h, i):
        to = seq_peer(i)
        return remote(
            qkv.at[:, :, head_cols(to, h)],
            vbuf.at[h, pl.ds(0, 3), rows_of(ms), :],
            v_send.at[i, h],
            v_recv.at[ms, h],
            {"seq": to},
        )

    def u_copy(h, i):
        to = seq_peer(i)
        return remote(
            cot.at[:, head_cols(to, h)],
            vbuf.at[h, 3, rows_of(ms), :],
            u_send.at[i, h],
            u_recv.at[ms, h],
            {"seq": to},
        )

    def send_head(h):
        for i in range(1, seq):
            v_copy(h, i).start()
            u_copy(h, i).start()

    def own_qkv(h):
        return pltpu.make_async_copy(
            qkv.at[:, :, head_cols(ms, h)],
            vbuf.at[h, pl.ds(0, 3), rows_of(ms), :],
            v_send.at[0, h],
        )

    def own_cot(h):
        return pltpu.make_async_copy(
            cot.at[:, head_cols(ms, h)], vbuf.at[h, 3, rows_of(ms), :], u_send.at[0, h]
        )

    def head_arrived(h):
        own_qkv(h).wait()
        own_cot(h).wait()
        for i in range(1, seq):
            s = seq_peer(i)
            remote(
                qkv.at[:, :, head_cols(s, h)],
                vbuf.at[h, pl.ds(0, 3), rows_of(s), :],
                v_send.at[i, h],
                v_recv.at[s, h],
                {"seq": s},
            ).wait_recv()
            remote(
                cot.at[:, head_cols(s, h)],
                vbuf.at[h, 3, rows_of(s), :],
                u_send.at[i, h],
                u_recv.at[s, h],
                {"seq": s},
            ).wait_recv()

    def r_copy(g, i):
        to = seq_peer(i)
        return remote(
            pbuf.at[to, g], rbuf.at[ms, g], r_send.at[i, g], r_recv.at[ms, g], {"seq": to}
        )

    def project(g, value):
        value = dot_nn(value, wbuf[...])
        for q in range(seq):
            pbuf[q, g] = value[q * part : (q + 1) * part].astype(BF)
        for i in range(1, seq):
            r_copy(g, i).start()

    send_head(0)
    local_x.wait()
    local_w.wait()
    project(md, xall[md])
    x_arrived(partner)
    project(partner, xall[partner])
    for h in range(1, FIRST):
        send_head(h)

    def step(k, carry):
        low = place - k
        high = place + k

        @pl.when(low >= 0)
        def _():
            g = 2 * low + core
            x_arrived(g)

            @pl.when(place + 1 < half)
            def _():
                hop(g, xall.at[g], True).start()

            forward(g, xall.at[g]).start()

        @pl.when(high < half)
        def _():
            g = 2 * high + core
            x_arrived(g)

            @pl.when(place > 0)
            def _():
                hop(g, xall.at[g], False).start()

            forward(g, xall.at[g]).start()

        @pl.when(low >= 0)
        def _():
            g = 2 * low + core
            project(g, xall[g])
            x_arrived(2 * low + 1 - core)
            project(2 * low + 1 - core, xall[2 * low + 1 - core])

        @pl.when(high < half)
        def _():
            g = 2 * high + core
            project(g, xall[g])
            x_arrived(2 * high + 1 - core)
            project(2 * high + 1 - core, xall[2 * high + 1 - core])

        return carry

    lax.fori_loop(1, half, step, 0)
    for h in range(FIRST, SECOND):
        send_head(h)

    def reduce_step(g, carry):
        total = pbuf[ms, g].astype(F32)
        for i in range(1, seq):
            s = seq_peer(i)
            remote(
                pbuf.at[s, g], rbuf.at[s, g], r_send.at[i, g], r_recv.at[s, g], {"seq": s}
            ).wait_recv()
            total = total + rbuf[s, g].astype(F32)
        sums[g] = total.astype(BF)
        return carry

    lax.fori_loop(0, dp, reduce_step, 0)

    goal = md // per
    slot = lax.rem(md, per)

    def z_copy(c):
        return remote(
            zsend.at[c], tbuf.at[ms, slot], z_send.at[c], t_recv.at[ms, slot], {"seq": goal, "dp": c}
        )

    def z_step(n, carry):
        c = dp_peer(n)
        zsend[c] = sums[source[c]]
        z_copy(c).start()
        return carry

    lax.fori_loop(1, dp, z_step, 0)
    zsend[md] = sums[source[md]]

    @pl.when(goal == ms)
    def _():
        tbuf[ms, slot] = zsend[md]

    @pl.when(goal != ms)
    def _():
        z_copy(md).start()

    for h in range(SECOND, heads):
        send_head(h)
    for h in range(heads):
        own_qkv(h).start()
        own_cot(h).start()

    def t_arrived(s, k):
        @pl.when((s != ms) | (ms * per + k != md))
        def _():
            remote(
                zsend.at[0], tbuf.at[s, k], z_send.at[0], t_recv.at[s, k], {"seq": seq_peer(1)}
            ).wait_recv()

    for s in range(seq):
        for k in range(per):
            t_arrived(s, k)
    for s in range(seq):
        for k in range(per):
            tfull[s * part : (s + 1) * part, k * cols : (k + 1) * cols] = tbuf[s, k].astype(F32)

    rows = tokens + prompt
    scale = 1.0 / math.sqrt(hd)
    valid = lax.broadcasted_iota(jnp.int32, (prompt, blk), 0) < length[0]

    def inverse(x):
        return lax.rsqrt(jnp.mean(x * x, axis=-1, keepdims=True) + EPS)

    def norm_back(x, r, gain, grad):
        scaled = grad * gain
        inner = jnp.mean(scaled * x, axis=-1, keepdims=True)
        return r * scaled - x * (r * r * r * inner)

    def o_copy(h, i):
        to = seq_peer(i)
        return remote(
            gbuf.at[h, :, rows_of(to), :],
            out.at[:, :, pl.ds(pl.multiple_of(ms * width + h * hd, hd), hd)],
            o_send.at[i, h],
            o_recv.at[ms, h],
            {"seq": to},
        )

    def o_local(h):
        return pltpu.make_async_copy(
            gbuf.at[h, :, rows_of(ms), :],
            out.at[:, :, pl.ds(pl.multiple_of(ms * width + h * hd, hd), hd)],
            o_send.at[0, h],
        )

    def text_local(h):
        at = pl.ds(pl.multiple_of(h * 3 * hd, 3 * hd), 3 * hd)
        return pltpu.make_async_copy(text_s.at[:, at], out_text.at[:, at], text_sem.at[h])

    def head(h, carry):
        mine = pl.ds(pl.multiple_of(h * hd, hd), hd)

        def text_cols(j):
            return pl.ds(pl.multiple_of((h * 3 + j) * hd, hd), hd)

        def joint(j):
            return jnp.concatenate(
                [vbuf[h, j].astype(F32), tfull[:, text_cols(j)]], axis=0
            )

        head_arrived(h)
        gq = gain_q[pl.ds(h, 1), :]
        gk = gain_k[pl.ds(h, 1), :]
        q = joint(0)
        k = joint(1)
        v = joint(2).astype(BF)
        qn_s[...] = (q * inverse(q) * gq).astype(BF)
        kn32 = (k * inverse(k) * gk).astype(BF).astype(F32)
        kn = kn32.astype(BF)
        kn_t = kn32.T.astype(BF)
        u_s[:tokens] = vbuf[h, 3]
        u_s[tokens:] = up_s[:, mine]

        def block(n, first):
            at = pl.ds(pl.multiple_of(n * blk, blk), blk)
            qb = qn_s[at, :]
            ub = u_s[at, :]
            e = jnp.exp2(dot_nt(kn, qb) * (scale * math.log2(math.e)))
            e = jnp.concatenate([e[:tokens], jnp.where(valid, e[tokens:], 0.0)], axis=0)
            probs = e * (1.0 / jnp.sum(e, axis=0, keepdims=True))
            grad_probs = dot_nt(v, ub)
            delta = jnp.sum(probs * grad_probs, axis=0, keepdims=True)
            grad_scores = (probs * (grad_probs - delta) * scale).astype(BF)
            dv = dot_nn(probs.astype(BF), ub)
            dk = dot_nn(grad_scores, qb)
            dq_s[at, :] = dot_nn(kn_t, grad_scores).T
            if first:
                dk_s[...] = dk
                dv_s[...] = dv
            else:
                dk_s[...] += dk
                dv_s[...] += dv

        block(0, True)
        if rows > blk:
            lax.fori_loop(1, rows // blk, lambda n, c: (block(n, False), c)[1], 0)
        grads = (
            norm_back(q, inverse(q), gq, dq_s[...]),
            norm_back(k, inverse(k), gk, dk_s[...]),
            dv_s[...],
        )
        for j in range(3):
            gbuf[h, j] = grads[j][:tokens].astype(BF)
            text_s[:, text_cols(j)] = grads[j][tokens:].astype(BF)
        for i in range(1, seq):
            o_copy(h, i).start()
        o_local(h).start()
        text_local(h).start()
        return carry

    local_u.wait()
    lax.fori_loop(0, heads, head, 0)

    def finish(h, carry):
        o_local(h).wait()
        text_local(h).wait()
        for i in range(1, seq):
            s = seq_peer(i)
            o_copy(h, i).wait_send()
            remote(
                gbuf.at[h, :, rows_of(s), :],
                out.at[:, :, pl.ds(pl.multiple_of(s * width + h * hd, hd), hd)],
                o_send.at[i, h],
                o_recv.at[s, h],
                {"seq": s},
            ).wait_recv()
        return carry

    lax.fori_loop(0, heads, finish, 0)

    def forward_wait(g):
        @pl.when(lax.rem(g, 2) == core)
        def _():
            forward(g, xall.at[g]).wait_send()
            at = g // 2

            @pl.when((at <= place) & (place + 1 < half))
            def _():
                hop(g, xall.at[g], True).wait_send()

            @pl.when((at >= place) & (place > 0))
            def _():
                hop(g, xall.at[g], False).wait_send()

    def drain(n, carry):
        for i in range(1, seq):
            r_copy(n, i).wait_send()
        forward_wait(n)
        return carry

    lax.fori_loop(0, dp, drain, 0)
    for n in range(1, dp):
        z_copy(dp_peer(n)).wait_send()

    @pl.when(goal != ms)
    def _():
        z_copy(md).wait_send()

    for i in range(1, seq):
        for h in range(heads):
            v_copy(h, i).wait_send()
            u_copy(h, i).wait_send()


def hand_over(video, text, video_out, text_out, sems):
    moves = [
        pltpu.make_async_copy(video.at[j], video_out.at[j], sems.at[j]) for j in range(3)
    ] + [pltpu.make_async_copy(text, text_out, sems.at[3])]
    for move in moves:
        move.start()
    for move in moves:
        move.wait()


def shards(
    seq,
    dp,
    video_qkv,
    video_cotangent,
    prompt_states,
    text_weight,
    text_cotangent,
    gain_query,
    gain_key,
    prompt_lengths,
    prompt_source,
):
    heads, hd = gain_query.shape
    tok = video_qkv.shape[1]
    every = video_qkv.shape[3]
    tokens = tok * seq
    prompt, feat = prompt_states.shape[1:]
    cols = text_weight.shape[1]
    part = prompt // seq
    per = dp // seq
    rows = tokens + prompt
    blk = rows if rows <= 640 else prompt
    width = heads * hd
    dma = pltpu.SemaphoreType.DMA
    hbm = pl.BlockSpec(memory_space=pl.ANY)
    vmem = pl.BlockSpec(memory_space=pltpu.VMEM)
    smem = pl.BlockSpec(memory_space=pltpu.SMEM)
    grad_video, grad_text = pl.pallas_call(
        functools.partial(kernel, seq, dp, blk),
        out_shape=(
            jax.ShapeDtypeStruct((3, tok, every), BF),
            jax.ShapeDtypeStruct((prompt, 3 * width), BF),
        ),
        in_specs=[hbm, hbm, hbm, hbm, hbm, vmem, vmem, smem, smem],
        out_specs=(hbm, hbm),
        scratch_shapes=[
            pltpu.VMEM((dp, prompt, feat), BF),
            pltpu.VMEM((feat, cols), BF),
            pltpu.VMEM((heads, 4, tokens, hd), BF),
            pltpu.VMEM((seq, dp, part, cols), BF),
            pltpu.VMEM((seq, dp, part, cols), BF),
            pltpu.VMEM((dp, part, cols), BF),
            pltpu.VMEM((dp, part, cols), BF),
            pltpu.VMEM((seq, per, part, cols), BF),
            pltpu.VMEM((prompt, per * cols), F32),
            pltpu.VMEM((rows, hd), BF),
            pltpu.VMEM((rows, hd), BF),
            pltpu.VMEM((rows, hd), F32),
            pltpu.VMEM((rows, hd), F32),
            pltpu.VMEM((rows, hd), F32),
            pltpu.VMEM((heads, 3, tokens, hd), BF),
            pltpu.VMEM((prompt, width), BF),
            pltpu.VMEM((prompt, 3 * width), BF),
            dma((dp,)),
            dma((dp,)),
            dma((dp,)),
            dma((dp,)),
            dma((seq, heads)),
            dma((seq, heads)),
            dma((seq, heads)),
            dma((seq, heads)),
            dma((seq, dp)),
            dma((seq, dp)),
            dma((dp,)),
            dma((seq, per)),
            dma((seq, heads)),
            dma((seq, heads)),
            dma((4,)),
            dma((heads,)),
        ],
        compiler_params=pltpu.CompilerParams(
            collective_id=0, has_side_effects=True, vmem_limit_bytes=56 * 1024 * 1024
        ),
    )(
        jnp.transpose(video_qkv[0], (1, 0, 2)),
        video_cotangent[0],
        prompt_states[0],
        text_weight,
        text_cotangent[0],
        gain_query,
        gain_key,
        prompt_lengths,
        prompt_source,
    )
    grad_video, grad_text = pl.pallas_call(
        hand_over,
        out_shape=(
            jax.ShapeDtypeStruct(grad_video.shape, BF),
            jax.ShapeDtypeStruct(grad_text.shape, BF),
        ),
        in_specs=[vmem, vmem],
        out_specs=(hbm, hbm),
        scratch_shapes=[dma((4,))],
    )(grad_video, grad_text)
    return jnp.transpose(grad_video, (1, 0, 2))[None], grad_text[None]


def solution(mesh):
    in_specs = (
        P("dp", "seq", None, None),
        P("dp", "seq", None),
        P("dp", None, "seq"),
        P("seq", "dp"),
        P("dp", None, "seq"),
        P("seq", None),
        P("seq", None),
        P("dp"),
        P(),
    )
    out_specs = (P("dp", "seq", None, None), P("dp", None, "seq"))
    body = functools.partial(shards, mesh.shape["seq"], mesh.shape["dp"])
    return jax.shard_map(body, mesh=mesh, in_specs=in_specs, out_specs=out_specs, check_vma=False)
```
